256 devices in a mesh: dp: 4 (over x), tensor: 4 (over y), expert: 16 (over z, core).
Axes of the slice: x: 4, y: 4, z: 8, core: 2. Of those that a mesh axis runs over, the one named last changes fastest.
Arguments:
- tokens: bfloat16 [8192, 5120], P(('dp', 'expert')), may hold values from -6 to 6
- expert_ids: int32 [8192, 1], P(('dp', 'expert')), may hold values from 0 to 15; in each aligned block of 128 rows (0 to 127, 128 to 255, ...) at most 10 rows name the same one
- norm_gain: float32 [5120], replicated, may hold values from 0.1 to 1.9
- router_weight: bfloat16 [5120, 16], replicated, may hold values from -0.078125 to 0.078125
- w_gate: bfloat16 [16, 5120, 6144], P(('dp', 'tensor'), None, 'expert'), may hold values from -0.15625 to 0.15625
- w_up: bfloat16 [16, 5120, 6144], P(('dp', 'tensor'), None, 'expert'), may hold values from -0.15625 to 0.15625
- w_down: bfloat16 [16, 6144, 5120], P(('dp', 'tensor'), 'expert'), may hold values from -0.078125 to 0.078125
Outputs:
- mixed: bfloat16 [8192, 5120], P(('dp', 'expert'))
The draws below stay inside these ranges and needn't reach their ends.
Inputs may be any that keep to these rules, and one draw needn't show every extreme that they name: `expert_ids`: within each aligned block of 128 rows (one group) no expert is named more than 10 times; in every draw some expert is named exactly 10 times in some block.
All inputs are finite; a program needn't handle non-finite values.
Results may differ from the reference program's by a relative error of at most 0.03.
Values may be sent and summed in bfloat16 or wider, within the bound.
No kernel may reach another device: no remote copies, remote signals or barrier semaphores. Data moves between devices by JAX's collectives and lax.ppermute only.
A program may use at most 128 MiB of HBM per device.

```python
import math
import jax
import jax.numpy as jnp
import numpy as np
from jax import lax

D = 5120
FF = 6144
TOK = 128
EXPERTS = 16
CAP = 10
TOKENS = 8192
N_EXPERT = 16


def block_scale(own_key, shape, pieces, smallest, high):
    def one(dim, shards_of):
        steps = jax.random.uniform(jax.random.fold_in(jax.random.fold_in(own_key, 6), dim), (shards_of,), jnp.float32, smallest / len(pieces), high / len(pieces))
        return jnp.repeat(jnp.exp(steps), shape[dim] // shards_of).reshape((-1,) + (1,) * (len(shape) - dim - 1))

    level = one(*pieces[0])
    for cut in pieces[1:]:
        level = level * one(*cut)
    return level


def assign_block(stream_key, own, number, rows, count, top, most, skew):
    order = jax.random.permutation(stream_key, count)
    packed, usual = portions_of(count, rows * top, most, skew, True), portions_of(count, rows * top, most, skew, False)
    places = jnp.arange(count)

    def named(tallies, turn):
        used = int((tallies > 0).sum())
        fixed = max(1, used // 4)
        moved = fixed + (places - fixed + turn * (used - fixed)) % max(1, count - fixed)
        return jnp.zeros((count,), jnp.int32).at[order[jnp.where(places < fixed, places, moved)]].set(jnp.asarray(tallies, jnp.int32))

    tallies = jnp.where(number % 4 == 0, named(packed, number // 4), named(usual, number - number // 4 - 1))
    mixed = jax.random.permutation(jax.random.fold_in(own, 3), count)
    donor, taker = mixed[0:count // 2 * 2:2], mixed[1:count // 2 * 2:2]
    room = jnp.minimum(tallies[donor] - 1, most - tallies[taker]) // 2
    room = jnp.where((donor == order[0]) | (taker == order[0]) | (tallies[taker] == 0), 0, jnp.maximum(room, 0))
    moved = jax.random.randint(jax.random.fold_in(own, 4), (count // 2,), 0, 1 << 20) % (room + 1)
    tallies = tallies.at[donor].add(-moved).at[taker].add(moved)
    items = jnp.searchsorted(jnp.cumsum(tallies), jnp.arange(rows * top), side="right").astype(jnp.int32)
    listing = items.reshape(top, rows).T
    listing = listing[jax.random.permutation(jax.random.fold_in(own, 1), rows)]
    turn = jax.random.randint(jax.random.fold_in(own, 2), (rows, 1), 0, top)
    return jnp.take_along_axis(listing, (jnp.arange(top)[None, :] + turn) % top, axis=1)


def portions_of(number_of, total, bound, lean, full):
    portions = [(1 << 20) // math.isqrt(grade ** lean) + 1 for grade in range(1, number_of + 1)]
    largest = bound if full else min(bound, max(-(-total // number_of), total * portions[0] // sum(portions)))
    least = 1 if total - largest >= number_of - 1 else 0
    given, spare = [largest] + [least] * (number_of - 1), total - largest - least * (number_of - 1)
    while spare > 0:
        movable = [i for i in range(1, number_of) if given[i] < largest] or [i for i in range(1, number_of) if given[i] < bound]
        whole, remaining = sum([portions[i] for i in movable]), spare
        for i in movable:
            addition = min(bound - given[i], max(1, remaining * portions[i] // whole), spare)
            given[i] = given[i] + addition
            spare = spare - addition
    return np.array(given)


def normal_values(rng, shape, scale, most, shards=(), kind=jnp.bfloat16):
    values = jax.random.normal(rng, shape, jnp.float32) * scale
    if len(shards) > 0:
        values = block_scale(rng, shape, shards, -0.22, 0.18) * values
    return jnp.clip(values, min=-most, max=most).astype(kind)


def setup_inputs(seed: int = 0) -> dict:
    key_list = jax.random.split(jax.random.key(seed), 8)
    tokens = normal_values(key_list[0], (TOKENS, D), 1.0, 6.0, ((0, 64),))
    expert_ids_keys = jax.random.split(jax.random.fold_in(key_list[1], 1), TOKENS // TOK)
    expert_ids_turns = jax.random.permutation(jax.random.fold_in(key_list[1], 3), TOKENS // TOK)
    expert_ids = jax.vmap(lambda own, number: assign_block(jax.random.fold_in(key_list[1], 2), own, number, TOK, EXPERTS, 1, CAP, 2))(expert_ids_keys, expert_ids_turns).reshape((TOKENS, 1))
    norm_gain = jnp.clip(1.0 + 0.18 * jax.random.normal(key_list[2], (D,), jnp.float32), 0.1, 1.9)
    router_weight = normal_values(key_list[3], (D, EXPERTS), D ** -0.5, 0.078125)
    w_gate = normal_values(key_list[4], (EXPERTS, D, FF), (D // 4) ** -0.5, 0.15625, ((0, 16), (2, 16)))
    w_up = normal_values(key_list[5], (EXPERTS, D, FF), (D // 4) ** -0.5, 0.15625, ((0, 16), (2, 16)))
    w_down = normal_values(key_list[6], (EXPERTS, FF, D), FF ** -0.5, 0.078125, ((0, 16), (1, 16)))
    return {"tokens": tokens, "expert_ids": expert_ids, "norm_gain": norm_gain, "router_weight": router_weight, "w_gate": w_gate, "w_up": w_up, "w_down": w_down}


def normalize(values, gain):
    widened = values.astype(jnp.float32)
    mean_square = lax.optimization_barrier(jnp.mean(widened * widened, axis=-1, keepdims=True))
    return (widened * lax.rsqrt(mean_square + 1e-05) * gain).astype(jnp.bfloat16)

def expert_apply(operands):
    slot_rows, gate_weight, up_weight, down_weight = operands
    gate_act = jnp.dot(slot_rows, gate_weight, preferred_element_type=jnp.float32)
    up_act = jnp.dot(slot_rows, up_weight, preferred_element_type=jnp.float32)
    hidden = (jax.nn.silu(gate_act) * up_act).astype(jnp.bfloat16)
    row_count = hidden.shape[0]
    piece = FF // N_EXPERT
    hidden_pieces = hidden.reshape(row_count, N_EXPERT, piece).astype(jnp.float32)
    down_pieces = down_weight.reshape(N_EXPERT, piece, D).astype(jnp.float32)
    partial_out = jnp.einsum('rnf,nfd->nrd', hidden_pieces, down_pieces).astype(jnp.bfloat16)
    return lax.optimization_barrier(jnp.sum(partial_out.astype(jnp.float32), axis=0)).astype(jnp.bfloat16)

def reference(tokens, expert_ids, norm_gain, router_weight, w_gate, w_up, w_down):
    normed = normalize(tokens, norm_gain)
    expert_of = expert_ids[:, 0].astype(jnp.int32)
    one_hot = expert_of[:, None] == jnp.arange(EXPERTS, dtype=jnp.int32)[None, :]
    logits = jnp.dot(normed, router_weight, preferred_element_type=jnp.float32)
    chosen_logit = lax.optimization_barrier(jnp.sum(jnp.where(one_hot, logits, jnp.float32(0.0)), axis=1))
    routed = (normed.astype(jnp.float32) * jax.nn.sigmoid(chosen_logit)[:, None]).astype(jnp.bfloat16)
    group_count = TOKENS // TOK
    grouped = one_hot.astype(jnp.int32).reshape(group_count, TOK, EXPERTS)
    slot_index = (lax.optimization_barrier(jnp.sum(jnp.cumsum(grouped, axis=1) * grouped, axis=2)) - 1).reshape(TOKENS).astype(jnp.int32)
    group_of = jnp.arange(TOKENS, dtype=jnp.int32) // TOK
    row_of = (group_of * CAP + slot_index).astype(jnp.int32)
    buffers = jnp.zeros((EXPERTS, group_count * CAP, D), jnp.bfloat16).at[expert_of, row_of].set(routed)
    outputs = lax.map(expert_apply, (buffers, w_gate, w_up, w_down))
    return outputs[expert_of, row_of]
```

```python
import jax
import jax.numpy as jnp
from jax import lax
from jax.sharding import PartitionSpec as P

BF16 = jnp.bfloat16
F32 = jnp.float32


def normalize(values, gain):
    widened = values.astype(F32)
    mean_square = jnp.mean(widened * widened, axis=-1, keepdims=True)
    return (widened * lax.rsqrt(mean_square + 1e-05) * gain).astype(BF16)


def add(*terms):
    total = terms[0].astype(F32)
    for term in terms[1:]:
        total = total + term.astype(F32)
    return total.astype(BF16)


def select_rows(row_of, row_count, values):
    picks = row_of[None, :] == jnp.arange(row_count, dtype=jnp.int32)[:, None]
    return jnp.dot(picks.astype(BF16), values, preferred_element_type=F32)


def shift(values, axis, steps):
    size = lax.axis_size(axis)
    return lax.ppermute(values, axis, [(i, (i + steps) % size) for i in range(size)])


def ring_step(values):
    size = lax.axis_size("expert")
    pairs = [(i, (i + (2 if i % 2 == 0 else -2)) % size) for i in range(size)]
    return lax.ppermute(values, "expert", pairs)


def swap(values):
    size = lax.axis_size("expert")
    return lax.ppermute(values, "expert", [(i, i ^ 1) for i in range(size)])


def per_device(tokens, expert_ids, norm_gain, router_weight, w_gate, w_up, w_down):
    dp_size = lax.axis_size("dp")
    tensor_size = lax.axis_size("tensor")
    chips = lax.axis_size("expert") // 2
    half = chips // 2
    token_count = tokens.shape[0]
    expert_count = dp_size * tensor_size
    capacity = 5 * token_count // (4 * expert_count)
    rows = dp_size * capacity
    my_dp = lax.axis_index("dp")
    my_tensor = lax.axis_index("tensor")
    gate, up, down = w_gate[0], w_up[0], w_down[0]

    normed = normalize(tokens, norm_gain)
    expert_of = expert_ids[:, 0]
    one_hot = expert_of[:, None] == jnp.arange(expert_count, dtype=jnp.int32)[None, :]
    logits = jnp.dot(normed, router_weight, preferred_element_type=F32)
    chosen_logit = jnp.sum(jnp.where(one_hot, logits, 0.0), axis=1)
    routed = (normed.astype(F32) * jax.nn.sigmoid(chosen_logit)[:, None]).astype(BF16)
    order = jnp.arange(token_count, dtype=jnp.int32)
    earlier = (expert_of[:, None] == expert_of[None, :]) & (order[:, None] < order[None, :])
    slot_index = jnp.sum(earlier.astype(jnp.int32), axis=0)
    ahead_dp = (expert_of // tensor_size - my_dp) % dp_size
    ahead_tensor = (expert_of % tensor_size - my_tensor) % tensor_size
    row_of = ahead_tensor * rows + ahead_dp * capacity + slot_index

    outgoing = select_rows(row_of, rows, routed).astype(BF16)
    arrived = [outgoing[:capacity]]
    for j in range(1, dp_size):
        arrived.append(shift(outgoing[j * capacity : (j + 1) * capacity], "dp", j))
    mine = jnp.concatenate(arrived, axis=0)

    def expert_apply(pieces):
        slot_rows = jnp.concatenate(pieces, axis=0)
        gate_act = jnp.dot(slot_rows, gate, preferred_element_type=F32)
        up_act = jnp.dot(slot_rows, up, preferred_element_type=F32)
        hidden = (jax.nn.silu(gate_act) * up_act).astype(BF16)
        return jnp.dot(hidden, down, preferred_element_type=F32).astype(BF16)

    other = swap(mine)
    partial = [expert_apply([mine, other])]
    far, near = mine, other
    for k in range(1, half):
        far, near = ring_step(far), ring_step(near)
        partial.append(expert_apply([far, near, swap(far), swap(near)]))
    far = ring_step(far)
    partial.append(expert_apply([far, swap(far)]))

    last = partial[half]
    far_sum = ring_step(add(last[:rows], swap(last[rows:])))
    near_sum = None
    for k in range(half - 1, 0, -1):
        part = partial[k]
        theirs = swap(part[: 2 * rows])
        near_terms = (part[2 * rows : 3 * rows], theirs[:rows])
        near_sum = ring_step(
            add(*near_terms) if near_sum is None else add(near_sum, *near_terms)
        )
        far_sum = ring_step(add(far_sum, part[3 * rows :], theirs[rows:]))
    slot_out = add(far_sum, partial[0][:rows], swap(add(near_sum, partial[0][rows:])))

    returned = [slot_out[:capacity]]
    for j in range(1, dp_size):
        returned.append(shift(slot_out[j * capacity : (j + 1) * capacity], "dp", -j))
    here = jnp.concatenate(returned, axis=0)
    ahead = shift(here, "tensor", -1)
    behind = shift(here, "tensor", 1)
    cut = rows // 16 * 8
    opposite = jnp.concatenate(
        [shift(ahead[:cut], "tensor", -1), shift(behind[cut:], "tensor", 1)], axis=0
    )
    held = jnp.concatenate([here, ahead, opposite, behind], axis=0)
    picks = row_of[:, None] == jnp.arange(tensor_size * rows, dtype=jnp.int32)[None, :]
    return jnp.dot(picks.astype(BF16), held, preferred_element_type=F32).astype(BF16)


def solution(mesh):
    return jax.shard_map(
        per_device,
        mesh=mesh,
        in_specs=(
            P(("dp", "expert"), None),
            P(("dp", "expert"), None),
            P(),
            P(),
            P(("dp", "tensor"), None, "expert"),
            P(("dp", "tensor"), None, "expert"),
            P(("dp", "tensor"), "expert", None),
        ),
        out_specs=P(("dp", "expert"), None),
        check_vma=False,
    )
```

```python
import functools

import jax
import jax.numpy as jnp
from jax import lax
from jax.experimental import pallas as pl
from jax.experimental.pallas import tpu as pltpu
from jax.sharding import PartitionSpec as P

BF16 = jnp.bfloat16
F32 = jnp.float32


def normalize(values, gain):
    widened = values.astype(F32)
    mean_square = jnp.mean(widened * widened, axis=-1, keepdims=True)
    return (widened * lax.rsqrt(mean_square + 1e-05) * gain).astype(BF16)


def add(*terms):
    total = terms[0].astype(F32)
    for term in terms[1:]:
        total = total + term.astype(F32)
    return total.astype(BF16)


def select_rows(row_of, row_count, values):
    picks = row_of[None, :] == jnp.arange(row_count, dtype=jnp.int32)[:, None]
    return jnp.dot(picks.astype(BF16), values, preferred_element_type=F32)


def shift(values, axis, steps):
    size = lax.axis_size(axis)
    return lax.ppermute(values, axis, [(i, (i + steps) % size) for i in range(size)])


def ring_step(values):
    size = lax.axis_size("expert")
    pairs = [(i, (i + (2 if i % 2 == 0 else -2)) % size) for i in range(size)]
    return lax.ppermute(values, "expert", pairs)


def swap(values):
    size = lax.axis_size("expert")
    return lax.ppermute(values, "expert", [(i, i ^ 1) for i in range(size)])


def expert_kernel(groups, step, *refs):
    count = sum(groups)
    pieces, (gate, up, down), outs = refs[:count], refs[count : count + 3], refs[count + 3 : -2]
    acts, hidden = refs[-2:]
    features, units = gate.shape
    acts[...] = jnp.zeros_like(acts)

    @pl.loop(0, features // step)
    def _(i):
        cols = pl.ds(pl.multiple_of(i * step, step), step)
        rows = jnp.concatenate([piece[:, cols].astype(F32) for piece in pieces], axis=0)
        weights = jnp.concatenate([gate[cols, :], up[cols, :]], axis=1)
        acts[...] += jnp.dot(rows.astype(BF16), weights, preferred_element_type=F32)

    gate_act, up_act = acts[:, :units], acts[:, units:]
    hidden[...] = (gate_act / (1.0 + jnp.exp(-gate_act)) * up_act).astype(BF16)

    @pl.loop(0, features // step)
    def _(i):
        cols = pl.ds(pl.multiple_of(i * step, step), step)
        product = jnp.dot(hidden[...], down[:, cols], preferred_element_type=F32)
        first = 0
        for out in outs:
            out[:, cols] = product[first : first + out.shape[0]].astype(BF16)
            first += out.shape[0]


def expert_apply(groups, pieces, gate, up, down):
    rows, features = pieces[0].shape
    total = rows * sum(groups)
    units = gate.shape[1]
    operands = [pltpu.with_memory_space_constraint(x, pltpu.VMEM) for x in (*pieces, gate, up, down)]
    return pl.pallas_call(
        functools.partial(expert_kernel, groups, 1024),
        out_shape=[pltpu.VMEM((rows * n, features), BF16) for n in groups],
        in_specs=[pl.BlockSpec(memory_space=pltpu.VMEM)] * len(operands),
        out_specs=[pl.BlockSpec(memory_space=pltpu.VMEM)] * len(groups),
        scratch_shapes=[pltpu.VMEM((total, 2 * units), F32), pltpu.VMEM((total, units), BF16)],
        compiler_params=pltpu.CompilerParams(vmem_limit_bytes=8 << 20),
        cost_estimate=pl.CostEstimate(
            flops=6 * total * features * units,
            bytes_accessed=6 * features * units + 4 * total * features,
            transcendentals=total * units,
        ),
    )(*operands)


def per_device(tokens, expert_ids, norm_gain, router_weight, w_gate, w_up, w_down):
    dp_size = lax.axis_size("dp")
    tensor_size = lax.axis_size("tensor")
    chips = lax.axis_size("expert") // 2
    half = chips // 2
    token_count = tokens.shape[0]
    expert_count = dp_size * tensor_size
    capacity = 5 * token_count // (4 * expert_count)
    rows = dp_size * capacity
    my_dp = lax.axis_index("dp")
    my_tensor = lax.axis_index("tensor")
    gate, up, down = w_gate[0], w_up[0], w_down[0]

    normed = normalize(tokens, norm_gain)
    expert_of = expert_ids[:, 0]
    one_hot = expert_of[:, None] == jnp.arange(expert_count, dtype=jnp.int32)[None, :]
    logits = jnp.dot(normed, router_weight, preferred_element_type=F32)
    chosen_logit = jnp.sum(jnp.where(one_hot, logits, 0.0), axis=1)
    routed = (normed.astype(F32) * jax.nn.sigmoid(chosen_logit)[:, None]).astype(BF16)
    order = jnp.arange(token_count, dtype=jnp.int32)
    earlier = (expert_of[:, None] == expert_of[None, :]) & (order[:, None] < order[None, :])
    slot_index = jnp.sum(earlier.astype(jnp.int32), axis=0)
    ahead_dp = (expert_of // tensor_size - my_dp) % dp_size
    ahead_tensor = (expert_of % tensor_size - my_tensor) % tensor_size
    row_of = ahead_tensor * rows + ahead_dp * capacity + slot_index

    outgoing = select_rows(row_of, rows, routed).astype(BF16)
    arrived = [outgoing[:capacity]]
    for j in range(1, dp_size):
        arrived.append(shift(outgoing[j * capacity : (j + 1) * capacity], "dp", j))
    mine = jnp.concatenate(arrived, axis=0)

    apply = functools.partial(expert_apply, gate=gate, up=up, down=down)
    other = swap(mine)
    own_part, other_part = apply((1, 1), [mine, other])
    far, near = ring_step(mine), ring_step(other)
    near, own_part = lax.optimization_barrier((near, own_part))
    parts = []
    for k in range(1, half):
        part = apply((2, 1, 1), [far, near, swap(far), swap(near)])
        far = ring_step(far)
        if k < half - 1:
            near = ring_step(near)
            near, part = lax.optimization_barrier((near, part))
        parts.append(part)
    last_kept, last_sent = apply((1, 1), [far, swap(far)])

    near_sum, far_sum = None, None
    for k in range(half - 1, 0, -1):
        sent, near_part, far_part = parts[k - 1]
        theirs = swap(sent)
        if near_sum is None:
            near_sum = ring_step(add(near_part, theirs[:rows]))
            far_sum = ring_step(add(last_kept, swap(last_sent)))
        else:
            near_sum = ring_step(add(near_sum, near_part, theirs[:rows]))
        far_sum = ring_step(add(far_sum, far_part, theirs[rows:]))
    slot_out = add(far_sum, own_part, swap(add(near_sum, other_part)))

    returned = [slot_out[:capacity]]
    for j in range(1, dp_size):
        returned.append(shift(slot_out[j * capacity : (j + 1) * capacity], "dp", -j))
    here = jnp.concatenate(returned, axis=0)
    ahead = shift(here, "tensor", -1)
    behind = shift(here, "tensor", 1)
    cut = rows // 16 * 8
    opposite = jnp.concatenate(
        [shift(ahead[:cut], "tensor", -1), shift(behind[cut:], "tensor", 1)], axis=0
    )
    held = jnp.concatenate([here, ahead, opposite, behind], axis=0)
    picks = row_of[:, None] == jnp.arange(tensor_size * rows, dtype=jnp.int32)[None, :]
    return jnp.dot(picks.astype(BF16), held, preferred_element_type=F32).astype(BF16)


def solution(mesh):
    return jax.shard_map(
        per_device,
        mesh=mesh,
        in_specs=(
            P(("dp", "expert"), None),
            P(("dp", "expert"), None),
            P(),
            P(),
            P(("dp", "tensor"), None, "expert"),
            P(("dp", "tensor"), None, "expert"),
            P(("dp", "tensor"), "expert", None),
        ),
        out_specs=P(("dp", "expert"), None),
        check_vma=False,
    )
```

```python
import functools

import jax
import jax.numpy as jnp
from jax import lax
from jax.experimental import pallas as pl
from jax.experimental.pallas import tpu as pltpu
from jax.sharding import PartitionSpec as P

BF16 = jnp.bfloat16
F32 = jnp.float32
I32 = jnp.int32
LANES = 128
VMEM_LIMIT = 8 << 20


def in_vmem(values):
    return pltpu.with_memory_space_constraint(values, pltpu.VMEM)


def vmem_specs(count):
    return [pl.BlockSpec(memory_space=pltpu.VMEM)] * count


def step_of(size, most):
    return max(s for s in range(LANES, most + 1, LANES) if size % s == 0)


def add(*terms):
    total = terms[0].astype(F32)
    for term in terms[1:]:
        total = total + term.astype(F32)
    return total.astype(BF16)


def shift(values, axis, steps):
    size = lax.axis_size(axis)
    return lax.ppermute(values, axis, [(i, (i + steps) % size) for i in range(size)])


def ring_step(values):
    size = lax.axis_size("expert")
    pairs = [(i, (i + (2 if i % 2 == 0 else -2)) % size) for i in range(size)]
    return lax.ppermute(values, "expert", pairs)


def swap(values):
    size = lax.axis_size("expert")
    return lax.ppermute(values, "expert", [(i, i ^ 1) for i in range(size)])


def route_kernel(sizes, place, tokens, ids_col, ids_row, gain, router, row_of, *outs):
    dp_size, tensor_size, capacity = sizes
    blocks, normed = outs[:-1], outs[-1]
    count, features = tokens.shape
    step = step_of(features, 512)
    spans = [pl.ds(i, step) for i in range(0, features, step)]

    total = jnp.zeros((count, LANES), F32)
    for i in range(0, features, LANES):
        part = tokens[:, i : i + LANES].astype(F32)
        total = total + part * part
    scale = lax.rsqrt(jnp.sum(total, axis=1, keepdims=True) * (1.0 / features) + 1e-05)

    logits = jnp.zeros((count, router.shape[0]), F32)
    for cols in spans:
        part = (tokens[:, cols].astype(F32) * scale * gain[:, cols]).astype(BF16)
        normed[:, cols] = part
        logits = logits + lax.dot_general(
            part, router[:, cols], (((1,), (1,)), ((), ())), preferred_element_type=F32
        )
    expert = lax.broadcasted_iota(I32, logits.shape, 1)
    chosen = jnp.sum(jnp.where(ids_col[...] == expert, logits, 0.0), axis=1, keepdims=True)
    gate = 1.0 / (1.0 + jnp.exp(-chosen))

    down = lax.broadcasted_iota(I32, (count, count), 0)
    across = lax.broadcasted_iota(I32, (count, count), 1)
    same = ids_col[...] == ids_row[...]
    slot_col = jnp.sum(jnp.where(same & (across < down), 1, 0), axis=1, keepdims=True)
    slot_row = jnp.sum(jnp.where(same & (down < across), 1, 0), axis=0, keepdims=True)

    def ahead(ids):
        dp_of = jnp.zeros_like(ids)
        for d in range(1, dp_size):
            dp_of = dp_of + jnp.where(ids >= d * tensor_size, 1, 0)
        on_dp = dp_of - place[0]
        on_tensor = ids - dp_of * tensor_size - place[1]
        on_dp = jnp.where(on_dp < 0, on_dp + dp_size, on_dp)
        return on_dp, jnp.where(on_tensor < 0, on_tensor + tensor_size, on_tensor)

    on_dp, on_tensor = ahead(ids_col[...])
    row_of[...] = (on_tensor * dp_size + on_dp) * capacity + slot_col
    on_dp, on_tensor = ahead(ids_row[...])
    padded = -(-capacity // 16) * 16
    target = jnp.where(on_tensor == 0, on_dp * padded + slot_row, -1)
    row = lax.broadcasted_iota(I32, (dp_size * padded, count), 0)
    picks = jnp.where(row == target, 1.0, 0.0).astype(BF16)
    for cols in spans:
        routed = (normed[:, cols].astype(F32) * gate).astype(BF16)
        product = jnp.dot(picks, routed, preferred_element_type=F32)
        for j, block in enumerate(blocks):
            block[:, cols] = product[j * padded : j * padded + capacity].astype(BF16)


def route(sizes, place, tokens, expert_ids, norm_gain, router_weight):
    count, features = tokens.shape
    dp_size, _, capacity = sizes
    operands = (
        tokens,
        expert_ids,
        expert_ids.reshape(1, count),
        norm_gain.reshape(1, features),
        router_weight.T,
    )
    return pl.pallas_call(
        functools.partial(route_kernel, sizes),
        out_shape=[pltpu.VMEM((count, 1), I32)]
        + [pltpu.VMEM((capacity, features), BF16)] * dp_size,
        in_specs=[pl.BlockSpec(memory_space=pltpu.SMEM)] + vmem_specs(len(operands)),
        out_specs=vmem_specs(1 + dp_size),
        scratch_shapes=[pltpu.VMEM((count, features), BF16)],
        compiler_params=pltpu.CompilerParams(vmem_limit_bytes=VMEM_LIMIT),
    )(place, *map(in_vmem, operands))


def load_kernel(*refs):
    count = len(refs) // 2
    sems = refs[-1]
    copies = [
        pltpu.make_async_copy(refs[i], refs[count + i], sems.at[i]) for i in range(count)
    ]
    for copy in copies:
        copy.start()
    for copy in copies:
        copy.wait()


def load(*arrays):
    return pl.pallas_call(
        load_kernel,
        out_shape=[pltpu.VMEM(x.shape, x.dtype) for x in arrays],
        in_specs=[pl.BlockSpec(memory_space=pl.ANY)] * len(arrays),
        out_specs=vmem_specs(len(arrays)),
        scratch_shapes=[pltpu.SemaphoreType.DMA((len(arrays),))],
        cost_estimate=pl.CostEstimate(
            flops=0, bytes_accessed=2 * sum(x.size * 2 for x in arrays), transcendentals=0
        ),
        compiler_params=pltpu.CompilerParams(vmem_limit_bytes=VMEM_LIMIT),
    )(*arrays)


def expert_kernel(groups, *refs):
    count = sum(groups)
    pieces, (gate, up, down), outs = refs[:count], refs[count : count + 3], refs[count + 3 : -2]
    acts, hidden = refs[-2:]
    features, units = gate.shape
    step = step_of(features, 1024)
    acts[...] = jnp.zeros_like(acts)

    @pl.loop(0, features // step)
    def _(i):
        cols = pl.ds(pl.multiple_of(i * step, step), step)
        rows = jnp.concatenate([piece[:, cols].astype(F32) for piece in pieces], axis=0)
        weights = jnp.concatenate([gate[cols, :], up[cols, :]], axis=1)
        acts[...] += jnp.dot(rows.astype(BF16), weights, preferred_element_type=F32)

    gate_act, up_act = acts[:, :units], acts[:, units:]
    hidden[...] = (gate_act / (1.0 + jnp.exp(-gate_act)) * up_act).astype(BF16)

    @pl.loop(0, features // step)
    def _(i):
        cols = pl.ds(pl.multiple_of(i * step, step), step)
        product = jnp.dot(hidden[...], down[:, cols], preferred_element_type=F32)
        first = 0
        for out in outs:
            out[:, cols] = product[first : first + out.shape[0]].astype(BF16)
            first += out.shape[0]


def expert_apply(groups, pieces, gate, up, down):
    rows, features = pieces[0].shape
    total = rows * sum(groups)
    units = gate.shape[1]
    operands = [in_vmem(x) for x in (*pieces, gate, up, down)]
    return pl.pallas_call(
        functools.partial(expert_kernel, groups),
        out_shape=[pltpu.VMEM((rows * n, features), BF16) for n in groups],
        in_specs=vmem_specs(len(operands)),
        out_specs=vmem_specs(len(groups)),
        scratch_shapes=[pltpu.VMEM((total, 2 * units), F32), pltpu.VMEM((total, units), BF16)],
        compiler_params=pltpu.CompilerParams(vmem_limit_bytes=VMEM_LIMIT),
        cost_estimate=pl.CostEstimate(
            flops=6 * total * features * units,
            bytes_accessed=6 * features * units + 4 * total * features,
            transcendentals=total * units,
        ),
    )(*operands)


def collect_kernel(row_of, *refs):
    pieces, (out, held, sems) = refs[:-3], refs[-3:]
    count, features = held.shape
    step = step_of(features, 1024)
    total = sum(piece.shape[0] for piece in pieces)
    across = lax.broadcasted_iota(I32, (count, total), 1)
    picks = jnp.where(row_of[...] == across, 1.0, 0.0).astype(BF16)
    copies = []
    for i in range(features // step):
        cols = pl.ds(i * step, step)
        rows = jnp.concatenate([piece[:, cols].astype(F32) for piece in pieces], axis=0)
        held[:, cols] = jnp.dot(picks, rows.astype(BF16), preferred_element_type=F32).astype(BF16)
        copies.append(pltpu.make_async_copy(held.at[:, cols], out.at[:, cols], sems.at[i]))
        copies[-1].start()
    for copy in copies:
        copy.wait()


def collect(row_of, pieces):
    count, features = row_of.shape[0], pieces[0].shape[1]
    return pl.pallas_call(
        collect_kernel,
        out_shape=jax.ShapeDtypeStruct((count, features), BF16),
        in_specs=vmem_specs(1 + len(pieces)),
        out_specs=pl.BlockSpec(memory_space=pl.ANY),
        scratch_shapes=[
            pltpu.VMEM((count, features), BF16),
            pltpu.SemaphoreType.DMA((features // step_of(features, 1024),)),
        ],
        compiler_params=pltpu.CompilerParams(vmem_limit_bytes=VMEM_LIMIT),
    )(*map(in_vmem, (row_of, *pieces)))


def after(values, *earlier):
    return lax.optimization_barrier((values, *earlier))[0]


def per_device(tokens, expert_ids, norm_gain, router_weight, w_gate, w_up, w_down):
    dp_size = lax.axis_size("dp")
    tensor_size = lax.axis_size("tensor")
    chips = lax.axis_size("expert") // 2
    half = chips // 2
    capacity = 5 * tokens.shape[0] // (4 * dp_size * tensor_size)
    rows = dp_size * capacity
    place = jnp.stack([lax.axis_index("dp"), lax.axis_index("tensor")]).astype(I32)

    row_of, *outgoing = route(
        (dp_size, tensor_size, capacity), place, tokens, expert_ids, norm_gain, router_weight
    )
    arrived = [outgoing[0]]
    for j in range(1, dp_size):
        arrived.append(shift(outgoing[j], "dp", j))
    gate, up, down = load(w_gate[0], w_up[0], w_down[0])
    arrived[-1] = after(arrived[-1], gate)
    mine = jnp.concatenate(arrived, axis=0)

    apply = functools.partial(expert_apply, gate=gate, up=up, down=down)
    other = swap(mine)
    own_part, other_part = apply((1, 1), [mine, other])
    far, near = after(ring_step(mine), own_part), ring_step(other)
    parts = []
    for k in range(1, half):
        part = apply((2, 1, 1), [far, near, swap(far), swap(near)])
        far = ring_step(far)
        if k < half - 1:
            near = after(ring_step(near), part[0])
        parts.append(part)
    last_kept, last_sent = apply((1, 1), [after(far, parts[-1][0]), swap(far)])

    near_sum, far_sum = None, None
    for k in range(half - 1, 0, -1):
        sent, near_part, far_part = parts[k - 1]
        theirs = swap(sent)
        if near_sum is None:
            near_term = add(near_part, theirs[:rows])
            far_sum = ring_step(add(last_kept, swap(last_sent)))
        else:
            near_term = add(near_sum, near_part, theirs[:rows])
        near_sum = ring_step(near_term)
        far_sum = ring_step(add(after(far_sum, near_term), far_part, theirs[rows:]))
    near_term = swap(add(near_sum, other_part))
    slot_out = add(after(far_sum, near_term), own_part, near_term)

    returned = [slot_out[:capacity]]
    for j in range(1, dp_size):
        returned.append(shift(slot_out[j * capacity : (j + 1) * capacity], "dp", -j))
    here = jnp.concatenate(returned, axis=0)
    ahead = shift(here, "tensor", -1)
    behind = shift(here, "tensor", 1)
    cut = rows // 16 * 8
    opposite = [shift(ahead[:cut], "tensor", -1), shift(behind[cut:], "tensor", 1)]
    return collect(row_of, [here, ahead, *opposite, behind])


def solution(mesh):
    return jax.shard_map(
        per_device,
        mesh=mesh,
        in_specs=(
            P(("dp", "expert"), None),
            P(("dp", "expert"), None),
            P(),
            P(),
            P(("dp", "tensor"), None, "expert"),
            P(("dp", "tensor"), None, "expert"),
            P(("dp", "tensor"), "expert", None),
        ),
        out_specs=P(("dp", "expert"), None),
        check_vma=False,
    )
```

```python
import functools

import jax
import jax.numpy as jnp
from jax import lax
from jax.experimental import pallas as pl
from jax.experimental.pallas import tpu as pltpu
from jax.sharding import PartitionSpec as P

BF16 = jnp.bfloat16
F32 = jnp.float32
I32 = jnp.int32
LANES = 128
VMEM_LIMIT = 8 << 20


def in_vmem(values):
    return pltpu.with_memory_space_constraint(values, pltpu.VMEM)


def in_hbm(values):
    return pltpu.with_memory_space_constraint(values, pltpu.HBM)


def vmem_specs(count):
    return [pl.BlockSpec(memory_space=pltpu.VMEM)] * count


def step_of(size, most):
    return max(s for s in range(LANES, most + 1, LANES) if size % s == 0)


def add(*terms):
    total = terms[0].astype(F32)
    for term in terms[1:]:
        total = total + term.astype(F32)
    return total.astype(BF16)


def shift(values, axis, steps):
    size = lax.axis_size(axis)
    return lax.ppermute(values, axis, [(i, (i + steps) % size) for i in range(size)])


def ring_step(values, name):
    size = lax.axis_size("expert")
    pairs = [(i, (i + (2 if i % 2 == 0 else -2)) % size) for i in range(size)]
    with jax.named_scope(name):
        return lax.ppermute(values, "expert", pairs)


def ring_leave(values, name):
    size = lax.axis_size("expert")
    pairs = [(i, (i + (3 if i % 2 == 0 else -3)) % size) for i in range(size)]
    with jax.named_scope(name):
        return lax.ppermute(values, "expert", pairs)


def swap(values):
    size = lax.axis_size("expert")
    with jax.named_scope("other_core"):
        return lax.ppermute(values, "expert", [(i, i ^ 1) for i in range(size)])


def route_kernel(sizes, place, *refs):
    dp_size, tensor_size, capacity = sizes
    sources, row_of, blocks = refs[:4], refs[4], refs[5 : 5 + dp_size]
    tokens, ids_row, gain, router, normed, sems = refs[5 + dp_size :]
    copies = [
        pltpu.make_async_copy(source, held, sems.at[i])
        for i, (source, held) in enumerate(zip(sources, (tokens, ids_row, gain, router)))
    ]
    for copy in copies:
        copy.start()
    for copy in copies:
        copy.wait()
    count, features = tokens.shape
    step = step_of(features, 512)
    spans = [pl.ds(i, step) for i in range(0, features, step)]
    down = lax.broadcasted_iota(I32, (count, count), 0)
    across = lax.broadcasted_iota(I32, (count, count), 1)
    ids_col = jnp.sum(jnp.where(down == across, ids_row[...], 0), axis=1, keepdims=True)

    total = jnp.zeros((count, LANES), F32)
    for i in range(0, features, LANES):
        part = tokens[:, i : i + LANES].astype(F32)
        total = total + part * part
    scale = lax.rsqrt(jnp.sum(total, axis=1, keepdims=True) * (1.0 / features) + 1e-05)

    logits = jnp.zeros((count, router.shape[0]), F32)
    for cols in spans:
        part = (tokens[:, cols].astype(F32) * scale * gain[:, cols]).astype(BF16)
        normed[:, cols] = part
        logits = logits + lax.dot_general(
            part, router[:, cols], (((1,), (1,)), ((), ())), preferred_element_type=F32
        )
    expert = lax.broadcasted_iota(I32, logits.shape, 1)
    chosen = jnp.sum(jnp.where(ids_col == expert, logits, 0.0), axis=1, keepdims=True)
    gate = 1.0 / (1.0 + jnp.exp(-chosen))

    same = ids_col == ids_row[...]
    slot_col = jnp.sum(jnp.where(same & (across < down), 1, 0), axis=1, keepdims=True)
    slot_row = jnp.sum(jnp.where(same & (down < across), 1, 0), axis=0, keepdims=True)

    def ahead(ids):
        dp_of = jnp.zeros_like(ids)
        for d in range(1, dp_size):
            dp_of = dp_of + jnp.where(ids >= d * tensor_size, 1, 0)
        on_dp = dp_of - place[0]
        on_tensor = ids - dp_of * tensor_size - place[1]
        on_dp = jnp.where(on_dp < 0, on_dp + dp_size, on_dp)
        return on_dp, jnp.where(on_tensor < 0, on_tensor + tensor_size, on_tensor)

    on_dp, on_tensor = ahead(ids_col)
    row_of[...] = (on_tensor * dp_size + on_dp) * capacity + slot_col
    on_dp, on_tensor = ahead(ids_row[...])
    padded = -(-capacity // 16) * 16
    target = jnp.where(on_tensor == 0, on_dp * padded + slot_row, -1)
    row = lax.broadcasted_iota(I32, (dp_size * padded, count), 0)
    picks = jnp.where(row == target, 1.0, 0.0).astype(BF16)
    for cols in spans:
        routed = (normed[:, cols].astype(F32) * gate).astype(BF16)
        product = jnp.dot(picks, routed, preferred_element_type=F32)
        for j, block in enumerate(blocks):
            block[:, cols] = product[j * padded : j * padded + capacity].astype(BF16)


def route(sizes, place, tokens, expert_ids, norm_gain, router_weight):
    count, features = tokens.shape
    dp_size, _, capacity = sizes
    operands = (
        tokens,
        expert_ids.reshape(1, count),
        norm_gain.reshape(1, features),
        router_weight.T,
    )
    return pl.pallas_call(
        functools.partial(route_kernel, sizes),
        out_shape=[pltpu.VMEM((count, 1), I32)]
        + [pltpu.VMEM((capacity, features), BF16)] * dp_size,
        in_specs=[pl.BlockSpec(memory_space=pltpu.SMEM)]
        + [pl.BlockSpec(memory_space=pl.ANY)] * len(operands),
        out_specs=vmem_specs(1 + dp_size),
        scratch_shapes=[pltpu.VMEM(x.shape, x.dtype) for x in operands]
        + [
            pltpu.VMEM((count, features), BF16),
            pltpu.SemaphoreType.DMA((len(operands),)),
        ],
        compiler_params=pltpu.CompilerParams(vmem_limit_bytes=VMEM_LIMIT),
    )(place, *map(in_hbm, operands))


def load_kernel(*refs):
    count = len(refs) // 2
    sems = refs[-1]
    copies = [
        pltpu.make_async_copy(refs[i], refs[count + i], sems.at[i]) for i in range(count)
    ]
    for copy in copies:
        copy.start()
    for copy in copies:
        copy.wait()


def load(*arrays):
    return pl.pallas_call(
        load_kernel,
        out_shape=[pltpu.VMEM(x.shape, x.dtype) for x in arrays],
        in_specs=[pl.BlockSpec(memory_space=pl.ANY)] * len(arrays),
        out_specs=vmem_specs(len(arrays)),
        scratch_shapes=[pltpu.SemaphoreType.DMA((len(arrays),))],
        compiler_params=pltpu.CompilerParams(vmem_limit_bytes=VMEM_LIMIT),
    )(*map(in_hbm, arrays))


def expert_kernel(groups, *refs):
    count = sum(groups)
    pieces, (gate, up, down), outs = refs[:count], refs[count : count + 3], refs[count + 3 : -2]
    acts, hidden = refs[-2:]
    features, units = gate.shape
    step = step_of(features, 1024)
    acts[...] = jnp.zeros_like(acts)

    @pl.loop(0, features // step)
    def _(i):
        cols = pl.ds(pl.multiple_of(i * step, step), step)
        rows = jnp.concatenate([piece[:, cols].astype(F32) for piece in pieces], axis=0)
        weights = jnp.concatenate([gate[cols, :], up[cols, :]], axis=1)
        acts[...] += jnp.dot(rows.astype(BF16), weights, preferred_element_type=F32)

    gate_act, up_act = acts[:, :units], acts[:, units:]
    hidden[...] = (gate_act / (1.0 + jnp.exp(-gate_act)) * up_act).astype(BF16)

    @pl.loop(0, features // step)
    def _(i):
        cols = pl.ds(pl.multiple_of(i * step, step), step)
        product = jnp.dot(hidden[...], down[:, cols], preferred_element_type=F32)
        first = 0
        for out in outs:
            out[:, cols] = product[first : first + out.shape[0]].astype(BF16)
            first += out.shape[0]


def expert_apply(groups, pieces, gate, up, down):
    rows, features = pieces[0].shape
    total = rows * sum(groups)
    units = gate.shape[1]
    operands = [in_vmem(x) for x in (*pieces, gate, up, down)]
    return pl.pallas_call(
        functools.partial(expert_kernel, groups),
        out_shape=[pltpu.VMEM((rows * n, features), BF16) for n in groups],
        in_specs=vmem_specs(len(operands)),
        out_specs=vmem_specs(len(groups)),
        scratch_shapes=[pltpu.VMEM((total, 2 * units), F32), pltpu.VMEM((total, units), BF16)],
        compiler_params=pltpu.CompilerParams(vmem_limit_bytes=VMEM_LIMIT),
    )(*operands)


def collect_kernel(row_of, *refs):
    pieces, (out, held, sems) = refs[:-3], refs[-3:]
    count, features = held.shape
    step = step_of(features, 1024)
    total = sum(piece.shape[0] for piece in pieces)
    across = lax.broadcasted_iota(I32, (count, total), 1)
    picks = jnp.where(row_of[...] == across, 1.0, 0.0).astype(BF16)
    copies = []
    for i in range(features // step):
        cols = pl.ds(i * step, step)
        rows = jnp.concatenate([piece[:, cols].astype(F32) for piece in pieces], axis=0)
        held[:, cols] = jnp.dot(picks, rows.astype(BF16), preferred_element_type=F32).astype(BF16)
        copies.append(pltpu.make_async_copy(held.at[:, cols], out.at[:, cols], sems.at[i]))
        copies[-1].start()
    for copy in copies:
        copy.wait()


def collect(row_of, pieces):
    count, features = row_of.shape[0], pieces[0].shape[1]
    return pl.pallas_call(
        collect_kernel,
        out_shape=jax.ShapeDtypeStruct((count, features), BF16),
        in_specs=vmem_specs(1 + len(pieces)),
        out_specs=pl.BlockSpec(memory_space=pl.ANY),
        scratch_shapes=[
            pltpu.VMEM((count, features), BF16),
            pltpu.SemaphoreType.DMA((features // step_of(features, 1024),)),
        ],
        compiler_params=pltpu.CompilerParams(vmem_limit_bytes=VMEM_LIMIT),
    )(*map(in_vmem, (row_of, *pieces)))


def after(values, *earlier):
    return lax.optimization_barrier((values, *earlier))[0]


def per_device(tokens, expert_ids, norm_gain, router_weight, w_gate, w_up, w_down):
    dp_size = lax.axis_size("dp")
    tensor_size = lax.axis_size("tensor")
    chips = lax.axis_size("expert") // 2
    half = chips // 2
    capacity = 5 * tokens.shape[0] // (4 * dp_size * tensor_size)
    rows = dp_size * capacity
    place = jnp.stack([lax.axis_index("dp"), lax.axis_index("tensor")]).astype(I32)

    row_of, *outgoing = route(
        (dp_size, tensor_size, capacity), place, tokens, expert_ids, norm_gain, router_weight
    )
    arrived = [outgoing[0]]
    for j in range(1, dp_size):
        arrived.append(shift(outgoing[j], "dp", j))
    gate, up, down = load(w_gate[0], w_up[0], w_down[0])
    arrived[-1] = after(arrived[-1], gate)
    mine = jnp.concatenate(arrived, axis=0)

    apply = functools.partial(expert_apply, gate=gate, up=up, down=down)
    other = swap(mine)
    own_part, other_part = apply((1, 1), [mine, other])
    base = (own_part, swap(other_part))
    far, near = after(ring_step(mine, "far_rows"), own_part), ring_step(other, "near_rows")
    near_terms, far_terms = [], []
    for k in range(1, half - 1):
        far_out, near_out, near_part, far_part = apply(
            (1, 1, 1, 1), [far, near, swap(far), swap(near)]
        )
        far = after(ring_step(far, "far_rows"), near, *(near_terms + far_terms)[-1:], *base)
        near = after(ring_step(near, "near_rows"), far_out)
        near_terms.append((near_part, swap(far_out)))
        far_terms.append((far_part, swap(near_out)))
    far_out, near_part = apply((1, 1), [far, swap(far)])
    far = after(ring_step(far, "far_rows"), near, far_out, *near_terms[-1], *far_terms[-1])
    near_terms.append((near_part, swap(far_out)))
    near_out, far_part, last_part, last_out = apply(
        (1, 1, 1, 1), [near, swap(near), after(far, *near_terms[-1]), swap(far)]
    )
    far_terms.append((far_part, swap(near_out)))

    far_sum, near_sum = add(last_part, swap(last_out)), None
    for k in range(half - 1, 0, -1):
        part, theirs = near_terms[k - 1]
        part = after(part, far_sum)
        near_sum = add(part, theirs) if near_sum is None else add(near_sum, part, theirs)
        near_sum = (ring_step if k > 1 else ring_leave)(near_sum, "near_sum")
        far_sum = add(ring_step(far_sum, "far_sum"), *far_terms[k - 1])
    slot_out = add(ring_step(far_sum, "far_sum"), near_sum, *base)

    returned = [slot_out[:capacity]]
    for j in range(1, dp_size):
        returned.append(shift(slot_out[j * capacity : (j + 1) * capacity], "dp", -j))
    here = jnp.concatenate(returned, axis=0)
    ahead = shift(here, "tensor", -1)
    behind = shift(here, "tensor", 1)
    cut = rows // 16 * 8
    opposite = [shift(ahead[:cut], "tensor", -1), shift(behind[cut:], "tensor", 1)]
    return collect(row_of, [here, ahead, *opposite, behind])


def solution(mesh):
    return jax.shard_map(
        per_device,
        mesh=mesh,
        in_specs=(
            P(("dp", "expert"), None),
            P(("dp", "expert"), None),
            P(),
            P(),
            P(("dp", "tensor"), None, "expert"),
            P(("dp", "tensor"), None, "expert"),
            P(("dp", "tensor"), "expert", None),
        ),
        out_specs=P(("dp", "expert"), None),
        check_vma=False,
    )
```

```python
import functools

import jax
import jax.numpy as jnp
from jax import lax
from jax.experimental import pallas as pl
from jax.experimental.pallas import tpu as pltpu
from jax.sharding import PartitionSpec as P

BF16 = jnp.bfloat16
F32 = jnp.float32
I32 = jnp.int32
LANES = 128
VMEM_LIMIT = 8 << 20


def in_vmem(values):
    return pltpu.with_memory_space_constraint(values, pltpu.VMEM)


def in_hbm(values):
    return pltpu.with_memory_space_constraint(values, pltpu.HBM)


def vmem_specs(count):
    return [pl.BlockSpec(memory_space=pltpu.VMEM)] * count


def step_of(size, most):
    return max(s for s in range(LANES, most + 1, LANES) if size % s == 0)


def add(*terms):
    total = terms[0].astype(F32)
    for term in terms[1:]:
        total = total + term.astype(F32)
    return total.astype(BF16)


def shift(values, axis, steps):
    size = lax.axis_size(axis)
    return lax.ppermute(values, axis, [(i, (i + steps) % size) for i in range(size)])


def ring_step(values, name):
    size = lax.axis_size("expert")
    pairs = [(i, (i + (2 if i % 2 == 0 else -2)) % size) for i in range(size)]
    with jax.named_scope(name):
        return lax.ppermute(values, "expert", pairs)


def ring_leave(values, name):
    size = lax.axis_size("expert")
    pairs = [(i, (i + (3 if i % 2 == 0 else -3)) % size) for i in range(size)]
    with jax.named_scope(name):
        return lax.ppermute(values, "expert", pairs)


def tensor_step(values):
    size, tensor_size = lax.axis_size("expert"), lax.axis_size("tensor")
    pairs = [
        (t * size + i, (t + (1 if i % 2 == 0 else -1)) % tensor_size * size + i)
        for t in range(tensor_size)
        for i in range(size)
    ]
    return lax.ppermute(values, ("tensor", "expert"), pairs)


def swap(values):
    size = lax.axis_size("expert")
    with jax.named_scope("other_core"):
        return lax.ppermute(values, "expert", [(i, i ^ 1) for i in range(size)])


def route_kernel(sizes, place, *refs):
    dp_size, tensor_size, capacity = sizes
    sources, row_of, packed = refs[:4], refs[4], refs[5]
    tokens, ids_row, gain, router, normed, sems = refs[6:]
    copies = [
        pltpu.make_async_copy(source, held, sems.at[i])
        for i, (source, held) in enumerate(zip(sources, (tokens, ids_row, gain, router)))
    ]
    for copy in copies:
        copy.start()
    for copy in copies:
        copy.wait()
    count, features = tokens.shape
    step = step_of(features, 512)
    spans = [pl.ds(i, step) for i in range(0, features, step)]
    down = lax.broadcasted_iota(I32, (count, count), 0)
    across = lax.broadcasted_iota(I32, (count, count), 1)
    ids_col = jnp.sum(jnp.where(down == across, ids_row[...], 0), axis=1, keepdims=True)

    total = jnp.zeros((count, LANES), F32)
    for i in range(0, features, LANES):
        part = tokens[:, i : i + LANES].astype(F32)
        total = total + part * part
    scale = lax.rsqrt(jnp.sum(total, axis=1, keepdims=True) * (1.0 / features) + 1e-05)

    logits = jnp.zeros((count, router.shape[0]), F32)
    for cols in spans:
        part = (tokens[:, cols].astype(F32) * scale * gain[:, cols]).astype(BF16)
        normed[:, cols] = part
        logits = logits + lax.dot_general(
            part, router[:, cols], (((1,), (1,)), ((), ())), preferred_element_type=F32
        )
    expert = lax.broadcasted_iota(I32, logits.shape, 1)
    chosen = jnp.sum(jnp.where(ids_col == expert, logits, 0.0), axis=1, keepdims=True)
    gate = 1.0 / (1.0 + jnp.exp(-chosen))

    same = ids_col == ids_row[...]
    slot_col = jnp.sum(jnp.where(same & (across < down), 1, 0), axis=1, keepdims=True)
    slot_row = jnp.sum(jnp.where(same & (down < across), 1, 0), axis=0, keepdims=True)

    def ahead(ids):
        dp_of = jnp.zeros_like(ids)
        for d in range(1, dp_size):
            dp_of = dp_of + jnp.where(ids >= d * tensor_size, 1, 0)
        on_dp = dp_of - place[0]
        on_tensor = (ids - dp_of * tensor_size - place[1]) * place[2]
        on_dp = jnp.where(on_dp < 0, on_dp + dp_size, on_dp)
        return on_dp, jnp.where(on_tensor < 0, on_tensor + tensor_size, on_tensor)

    on_dp, on_tensor = ahead(ids_col)
    row_of[...] = (on_tensor * dp_size + on_dp) * capacity + slot_col
    on_dp, on_tensor = ahead(ids_row[...])
    target = jnp.where(on_tensor == 0, on_dp * capacity + slot_row, -1)
    row = lax.broadcasted_iota(I32, (packed.shape[0], count), 0)
    picks = jnp.where(row == target, 1.0, 0.0).astype(BF16)
    for cols in spans:
        routed = (normed[:, cols].astype(F32) * gate).astype(BF16)
        packed[:, cols] = jnp.dot(picks, routed, preferred_element_type=F32).astype(BF16)


def route(sizes, place, tokens, expert_ids, norm_gain, router_weight):
    count, features = tokens.shape
    dp_size, _, capacity = sizes
    operands = (
        tokens,
        expert_ids.reshape(1, count),
        norm_gain.reshape(1, features),
        router_weight.T,
    )
    return pl.pallas_call(
        functools.partial(route_kernel, sizes),
        out_shape=[
            pltpu.VMEM((count, 1), I32),
            pltpu.VMEM((dp_size * capacity, features), BF16),
        ],
        in_specs=[pl.BlockSpec(memory_space=pltpu.SMEM)]
        + [pl.BlockSpec(memory_space=pl.ANY)] * len(operands),
        out_specs=vmem_specs(2),
        scratch_shapes=[pltpu.VMEM(x.shape, x.dtype) for x in operands]
        + [
            pltpu.VMEM((count, features), BF16),
            pltpu.SemaphoreType.DMA((len(operands),)),
        ],
        compiler_params=pltpu.CompilerParams(vmem_limit_bytes=VMEM_LIMIT),
    )(place, *map(in_hbm, operands))


def load_kernel(*refs):
    count = len(refs) // 2
    sems = refs[-1]
    copies = [
        pltpu.make_async_copy(refs[i], refs[count + i], sems.at[i]) for i in range(count)
    ]
    for copy in copies:
        copy.start()
    for copy in copies:
        copy.wait()


def load(*arrays):
    return pl.pallas_call(
        load_kernel,
        out_shape=[pltpu.VMEM(x.shape, x.dtype) for x in arrays],
        in_specs=[pl.BlockSpec(memory_space=pl.ANY)] * len(arrays),
        out_specs=vmem_specs(len(arrays)),
        scratch_shapes=[pltpu.SemaphoreType.DMA((len(arrays),))],
        compiler_params=pltpu.CompilerParams(vmem_limit_bytes=VMEM_LIMIT),
    )(*map(in_hbm, arrays))


def expert_kernel(groups, *refs):
    count = sum(groups)
    pieces, (gate, up, down), outs = refs[:count], refs[count : count + 3], refs[count + 3 : -2]
    acts, hidden = refs[-2:]
    features, units = gate.shape
    step = step_of(features, 2560)
    acts[...] = jnp.zeros_like(acts)

    @pl.loop(0, features // step)
    def _(i):
        cols = pl.ds(pl.multiple_of(i * step, step), step)
        rows = jnp.concatenate([piece[:, cols].astype(F32) for piece in pieces], axis=0)
        weights = jnp.concatenate([gate[cols, :], up[cols, :]], axis=1)
        acts[...] += jnp.dot(rows.astype(BF16), weights, preferred_element_type=F32)

    gate_act, up_act = acts[:, :units], acts[:, units:]
    hidden[...] = (gate_act / (1.0 + jnp.exp(-gate_act)) * up_act).astype(BF16)

    @pl.loop(0, features // step)
    def _(i):
        cols = pl.ds(pl.multiple_of(i * step, step), step)
        product = jnp.dot(hidden[...], down[:, cols], preferred_element_type=F32)
        first = 0
        for out in outs:
            out[:, cols] = product[first : first + out.shape[0]].astype(BF16)
            first += out.shape[0]


def expert_apply(groups, pieces, gate, up, down):
    rows, features = pieces[0].shape
    total = rows * sum(groups)
    units = gate.shape[1]
    operands = [in_vmem(x) for x in (*pieces, gate, up, down)]
    return pl.pallas_call(
        functools.partial(expert_kernel, groups),
        out_shape=[pltpu.VMEM((rows * n, features), BF16) for n in groups],
        in_specs=vmem_specs(len(operands)),
        out_specs=vmem_specs(len(groups)),
        scratch_shapes=[pltpu.VMEM((total, 2 * units), F32), pltpu.VMEM((total, units), BF16)],
        compiler_params=pltpu.CompilerParams(vmem_limit_bytes=VMEM_LIMIT),
    )(*operands)


def collect_kernel(row_of, *refs):
    pieces, (out, held, sems) = refs[:-3], refs[-3:]
    count, features = held.shape
    step = step_of(features, 1024)
    total = sum(piece.shape[0] for piece in pieces)
    across = lax.broadcasted_iota(I32, (count, total), 1)
    picks = jnp.where(row_of[...] == across, 1.0, 0.0).astype(BF16)
    copies = []
    for i in range(features // step):
        cols = pl.ds(i * step, step)
        rows = jnp.concatenate([piece[:, cols].astype(F32) for piece in pieces], axis=0)
        held[:, cols] = jnp.dot(picks, rows.astype(BF16), preferred_element_type=F32).astype(BF16)
        copies.append(pltpu.make_async_copy(held.at[:, cols], out.at[:, cols], sems.at[i]))
        copies[-1].start()
    for copy in copies:
        copy.wait()


def collect(row_of, pieces):
    count, features = row_of.shape[0], pieces[0].shape[1]
    return pl.pallas_call(
        collect_kernel,
        out_shape=jax.ShapeDtypeStruct((count, features), BF16),
        in_specs=vmem_specs(1 + len(pieces)),
        out_specs=pl.BlockSpec(memory_space=pl.ANY),
        scratch_shapes=[
            pltpu.VMEM((count, features), BF16),
            pltpu.SemaphoreType.DMA((features // step_of(features, 1024),)),
        ],
        compiler_params=pltpu.CompilerParams(vmem_limit_bytes=VMEM_LIMIT),
    )(*map(in_vmem, (row_of, *pieces)))


def exchange(values, direction):
    size = lax.axis_size("dp")
    rows = values.shape[0] // size
    blocks = [values[j * rows : (j + 1) * rows] for j in range(size)]
    return blocks[:1] + [shift(blocks[j], "dp", direction * j) for j in range(1, size)]


def after(values, *earlier):
    return lax.optimization_barrier((values, *earlier))[0]


def per_device(tokens, expert_ids, norm_gain, router_weight, w_gate, w_up, w_down):
    dp_size = lax.axis_size("dp")
    tensor_size = lax.axis_size("tensor")
    chips = lax.axis_size("expert") // 2
    half = chips // 2
    capacity = 5 * tokens.shape[0] // (4 * dp_size * tensor_size)
    rows = dp_size * capacity
    core = lax.axis_index("expert") % 2
    place = jnp.stack([lax.axis_index("dp"), lax.axis_index("tensor"), 1 - 2 * core]).astype(I32)

    row_of, packed = route(
        (dp_size, tensor_size, capacity), place, tokens, expert_ids, norm_gain, router_weight
    )
    arrived = exchange(packed, 1)
    gate, up, down = load(w_gate[0], w_up[0], w_down[0])
    arrived[-1] = after(arrived[-1], gate)
    mine = jnp.concatenate(arrived, axis=0)
    far = ring_step(mine, "far_rows")

    apply = functools.partial(expert_apply, gate=gate, up=up, down=down)
    other = swap(mine)
    own_part, other_part = apply((1, 1), [mine, other])
    base = (own_part, swap(other_part))
    far, near = after(far, own_part), ring_step(other, "near_rows")
    near_terms, far_terms = [], []
    for k in range(1, half - 1):
        far_out, near_out, near_part, far_part = apply(
            (1, 1, 1, 1), [far, near, swap(far), swap(near)]
        )
        far = after(ring_step(far, "far_rows"), near, *(near_terms + far_terms)[-1:], *base)
        near = after(ring_step(near, "near_rows"), far_out)
        near_terms.append((near_part, swap(far_out)))
        far_terms.append((far_part, swap(near_out)))
    far_out, near_part = apply((1, 1), [far, swap(far)])
    far = after(ring_step(far, "far_rows"), near, far_out, *near_terms[-1], *far_terms[-1])
    near_terms.append((near_part, swap(far_out)))
    last_part, last_out = apply((1, 1), [after(far, *near_terms[-1]), swap(far)])
    far_sum = add(last_part, swap(last_out))
    near_out, far_part = apply((1, 1), [after(near, far_sum), swap(near)])
    far_terms.append((far_part, swap(near_out)))

    near_sum = None
    for k in range(half - 1, 0, -1):
        part, theirs = near_terms[k - 1]
        part = after(part, far_sum)
        near_sum = add(part, theirs) if near_sum is None else add(near_sum, part, theirs)
        near_sum = (ring_step if k > 1 else ring_leave)(near_sum, "near_sum")
        far_sum = add(ring_step(far_sum, "far_sum"), *far_terms[k - 1])
    slot_out = add(ring_step(far_sum, "far_sum"), near_sum, *base)

    here = jnp.concatenate(exchange(slot_out, -1), axis=0)
    far = tensor_step(here)
    near = swap(tensor_step(swap(here)))
    return collect(row_of, [here, near, tensor_step(far), far])


def solution(mesh):
    return jax.shard_map(
        per_device,
        mesh=mesh,
        in_specs=(
            P(("dp", "expert"), None),
            P(("dp", "expert"), None),
            P(),
            P(),
            P(("dp", "tensor"), None, "expert"),
            P(("dp", "tensor"), None, "expert"),
            P(("dp", "tensor"), "expert", None),
        ),
        out_specs=P(("dp", "expert"), None),
        check_vma=False,
    )
```

```python
import functools

import jax
import jax.numpy as jnp
from jax import lax
from jax.experimental import pallas as pl
from jax.experimental.pallas import tpu as pltpu
from jax.sharding import PartitionSpec as P

BF16 = jnp.bfloat16
F32 = jnp.float32
I32 = jnp.int32
LANES = 128
VMEM_LIMIT = 8 << 20


def in_vmem(values):
    return pltpu.with_memory_space_constraint(values, pltpu.VMEM)


def in_hbm(values):
    return pltpu.with_memory_space_constraint(values, pltpu.HBM)


def vmem_specs(count):
    return [pl.BlockSpec(memory_space=pltpu.VMEM)] * count


def step_of(size, most):
    return max(s for s in range(LANES, most + 1, LANES) if size % s == 0)


def add(*terms):
    total = terms[0].astype(F32)
    for term in terms[1:]:
        total = total + term.astype(F32)
    return total.astype(BF16)


def shift(values, axis, steps):
    size = lax.axis_size(axis)
    return lax.ppermute(values, axis, [(i, (i + steps) % size) for i in range(size)])


def ring_step(values, name):
    size = lax.axis_size("expert")
    pairs = [(i, (i + (2 if i % 2 == 0 else -2)) % size) for i in range(size)]
    with jax.named_scope(name):
        return lax.ppermute(values, "expert", pairs)


def ring_leave(values, name):
    size = lax.axis_size("expert")
    pairs = [(i, (i + (3 if i % 2 == 0 else -3)) % size) for i in range(size)]
    with jax.named_scope(name):
        return lax.ppermute(values, "expert", pairs)


def tensor_step(values):
    size, tensor_size = lax.axis_size("expert"), lax.axis_size("tensor")
    pairs = [
        (t * size + i, (t + (1 if i % 2 == 0 else -1)) % tensor_size * size + i)
        for t in range(tensor_size)
        for i in range(size)
    ]
    return lax.ppermute(values, ("tensor", "expert"), pairs)


def swap(values):
    size = lax.axis_size("expert")
    with jax.named_scope("other_core"):
        return lax.ppermute(values, "expert", [(i, i ^ 1) for i in range(size)])


def route_kernel(sizes, place, *refs):
    dp_size, tensor_size, capacity = sizes
    sources, row_of, packed = refs[:4], refs[4], refs[5]
    tokens, ids_row, gain, router, normed, sems = refs[6:]
    count, features = tokens.shape
    rows = packed.shape[0]
    step = step_of(features, 1280)
    spans = [pl.ds(i, step) for i in range(0, features, step)]
    part_size = step_of(features, 1280)
    part_spans = [pl.ds(i, part_size) for i in range(0, features, part_size)]
    copies = [
        pltpu.make_async_copy(source, held, sems.at[i])
        for i, (source, held) in enumerate(zip(sources[1:], (ids_row, gain, router)))
    ] + [
        pltpu.make_async_copy(sources[0].at[:, cols], tokens.at[:, cols], sems.at[3 + i])
        for i, cols in enumerate(part_spans)
    ]
    for copy in copies:
        copy.start()

    copies[0].wait()
    down = lax.broadcasted_iota(I32, (count, count), 0)
    across = lax.broadcasted_iota(I32, (count, count), 1)
    ids_col = jnp.sum(jnp.where(down == across, ids_row[...], 0), axis=1, keepdims=True)
    same = ids_col == ids_row[...]
    slot_col = jnp.sum(jnp.where(same & (across < down), 1, 0), axis=1, keepdims=True)
    slot_row = jnp.sum(jnp.where(same & (down < across), 1, 0), axis=0, keepdims=True)

    def ahead(ids):
        dp_of = jnp.zeros_like(ids)
        for d in range(1, dp_size):
            dp_of = dp_of + jnp.where(ids >= d * tensor_size, 1, 0)
        on_dp = dp_of - place[0]
        on_tensor = (ids - dp_of * tensor_size - place[1]) * place[2]
        on_dp = jnp.where(on_dp < 0, on_dp + dp_size, on_dp)
        return on_dp, jnp.where(on_tensor < 0, on_tensor + tensor_size, on_tensor)

    on_dp, on_tensor = ahead(ids_col)
    row_of[...] = (on_tensor * dp_size + on_dp) * capacity + slot_col
    on_dp, on_tensor = ahead(ids_row[...])
    target = jnp.where(on_tensor == 0, on_dp * capacity + slot_row, -1)
    row = lax.broadcasted_iota(I32, (rows, count), 0)
    picks = jnp.where(row == target, 1.0, 0.0).astype(BF16)

    total = jnp.zeros((rows, LANES), F32)
    for cols, copy in zip(part_spans, copies[3:]):
        copy.wait()
        part = jnp.dot(picks, tokens[:, cols], preferred_element_type=F32)
        normed[:, cols] = part.astype(BF16)
        for i in range(0, part_size, LANES):
            total = total + part[:, i : i + LANES] * part[:, i : i + LANES]
    scale = lax.rsqrt(jnp.sum(total, axis=1, keepdims=True) * (1.0 / features) + 1e-05)

    copies[1].wait()
    copies[2].wait()
    logits = jnp.zeros((rows, router.shape[0]), F32)
    for cols in spans:
        part = (normed[:, cols].astype(F32) * scale * gain[:, cols]).astype(BF16)
        normed[:, cols] = part
        logits = logits + lax.dot_general(
            part, router[:, cols], (((1,), (1,)), ((), ())), preferred_element_type=F32
        )
    row = lax.broadcasted_iota(I32, logits.shape, 0)
    dp_of = jnp.zeros_like(row) + place[0]
    for d in range(1, dp_size):
        dp_of = dp_of + jnp.where(row >= d * capacity, 1, 0)
    dp_of = jnp.where(dp_of >= dp_size, dp_of - dp_size, dp_of)
    expert = lax.broadcasted_iota(I32, logits.shape, 1)
    mine = expert == dp_of * tensor_size + place[1]
    chosen = jnp.sum(jnp.where(mine, logits, 0.0), axis=1, keepdims=True)
    gate = 1.0 / (1.0 + jnp.exp(-chosen))
    for cols in spans:
        packed[:, cols] = (normed[:, cols].astype(F32) * gate).astype(BF16)


def route(sizes, place, tokens, expert_ids, norm_gain, router_weight):
    count, features = tokens.shape
    dp_size, _, capacity = sizes
    operands = (
        tokens,
        expert_ids.reshape(1, count),
        norm_gain.reshape(1, features),
        router_weight.T,
    )
    return pl.pallas_call(
        functools.partial(route_kernel, sizes),
        out_shape=[
            pltpu.VMEM((count, 1), I32),
            pltpu.VMEM((dp_size * capacity, features), BF16),
        ],
        in_specs=[pl.BlockSpec(memory_space=pltpu.SMEM)]
        + [pl.BlockSpec(memory_space=pl.ANY)] * len(operands),
        out_specs=vmem_specs(2),
        scratch_shapes=[pltpu.VMEM(x.shape, x.dtype) for x in operands]
        + [
            pltpu.VMEM((dp_size * capacity, features), BF16),
            pltpu.SemaphoreType.DMA((3 + features // step_of(features, 1280),)),
        ],
        compiler_params=pltpu.CompilerParams(vmem_limit_bytes=VMEM_LIMIT),
    )(place, *map(in_hbm, operands))


def load_kernel(*refs):
    count = len(refs) // 2
    sems = refs[-1]
    copies = [
        pltpu.make_async_copy(refs[i], refs[count + i], sems.at[i]) for i in range(count)
    ]
    for copy in copies:
        copy.start()
    for copy in copies:
        copy.wait()


def load(*arrays):
    return pl.pallas_call(
        load_kernel,
        out_shape=[pltpu.VMEM(x.shape, x.dtype) for x in arrays],
        in_specs=[pl.BlockSpec(memory_space=pl.ANY)] * len(arrays),
        out_specs=vmem_specs(len(arrays)),
        scratch_shapes=[pltpu.SemaphoreType.DMA((len(arrays),))],
        compiler_params=pltpu.CompilerParams(vmem_limit_bytes=VMEM_LIMIT),
    )(*map(in_hbm, arrays))


def expert_kernel(groups, *refs):
    count = sum(groups)
    pieces, (gate, up, down), outs = refs[:count], refs[count : count + 3], refs[count + 3 : -2]
    acts, hidden = refs[-2:]
    features, units = gate.shape
    step = step_of(features, 2560)
    acts[...] = jnp.zeros_like(acts)

    @pl.loop(0, features // step)
    def _(i):
        cols = pl.ds(pl.multiple_of(i * step, step), step)
        rows = jnp.concatenate([piece[:, cols].astype(F32) for piece in pieces], axis=0)
        weights = jnp.concatenate([gate[cols, :], up[cols, :]], axis=1)
        acts[...] += jnp.dot(rows.astype(BF16), weights, preferred_element_type=F32)

    gate_act, up_act = acts[:, :units], acts[:, units:]
    hidden[...] = (gate_act / (1.0 + jnp.exp(-gate_act)) * up_act).astype(BF16)

    @pl.loop(0, features // step)
    def _(i):
        cols = pl.ds(pl.multiple_of(i * step, step), step)
        product = jnp.dot(hidden[...], down[:, cols], preferred_element_type=F32)
        first = 0
        for out in outs:
            out[:, cols] = product[first : first + out.shape[0]].astype(BF16)
            first += out.shape[0]


def expert_apply(groups, pieces, gate, up, down):
    rows, features = pieces[0].shape
    total = rows * sum(groups)
    units = gate.shape[1]
    operands = [in_vmem(x) for x in (*pieces, gate, up, down)]
    return pl.pallas_call(
        functools.partial(expert_kernel, groups),
        out_shape=[pltpu.VMEM((rows * n, features), BF16) for n in groups],
        in_specs=vmem_specs(len(operands)),
        out_specs=vmem_specs(len(groups)),
        scratch_shapes=[pltpu.VMEM((total, 2 * units), F32), pltpu.VMEM((total, units), BF16)],
        compiler_params=pltpu.CompilerParams(vmem_limit_bytes=VMEM_LIMIT),
    )(*operands)


def collect_kernel(row_of, *refs):
    pieces, (out, held, sems) = refs[:-3], refs[-3:]
    count, features = held.shape
    step = step_of(features, 1024)
    total = sum(piece.shape[0] for piece in pieces)
    across = lax.broadcasted_iota(I32, (count, total), 1)
    picks = jnp.where(row_of[...] == across, 1.0, 0.0).astype(BF16)
    copies = []
    for i in range(features // step):
        cols = pl.ds(i * step, step)
        rows = jnp.concatenate([piece[:, cols].astype(F32) for piece in pieces], axis=0)
        held[:, cols] = jnp.dot(picks, rows.astype(BF16), preferred_element_type=F32).astype(BF16)
        copies.append(pltpu.make_async_copy(held.at[:, cols], out.at[:, cols], sems.at[i]))
        copies[-1].start()
    for copy in copies:
        copy.wait()


def collect(row_of, pieces):
    count, features = row_of.shape[0], pieces[0].shape[1]
    return pl.pallas_call(
        collect_kernel,
        out_shape=jax.ShapeDtypeStruct((count, features), BF16),
        in_specs=vmem_specs(1 + len(pieces)),
        out_specs=pl.BlockSpec(memory_space=pl.ANY),
        scratch_shapes=[
            pltpu.VMEM((count, features), BF16),
            pltpu.SemaphoreType.DMA((features // step_of(features, 1024),)),
        ],
        compiler_params=pltpu.CompilerParams(vmem_limit_bytes=VMEM_LIMIT),
    )(*map(in_vmem, (row_of, *pieces)))


def exchange(values, direction):
    size = lax.axis_size("dp")
    rows = values.shape[0] // size
    blocks = [values[j * rows : (j + 1) * rows] for j in range(size)]
    return blocks[:1] + [shift(blocks[j], "dp", direction * j) for j in range(1, size)]


def after(values, *earlier):
    return lax.optimization_barrier((values, *earlier))[0]


def per_device(tokens, expert_ids, norm_gain, router_weight, w_gate, w_up, w_down):
    dp_size = lax.axis_size("dp")
    tensor_size = lax.axis_size("tensor")
    chips = lax.axis_size("expert") // 2
    half = chips // 2
    capacity = 5 * tokens.shape[0] // (4 * dp_size * tensor_size)
    rows = dp_size * capacity
    core = lax.axis_index("expert") % 2
    place = jnp.stack([lax.axis_index("dp"), lax.axis_index("tensor"), 1 - 2 * core]).astype(I32)

    row_of, packed = route(
        (dp_size, tensor_size, capacity), place, tokens, expert_ids, norm_gain, router_weight
    )
    arrived = exchange(packed, 1)
    gate, up, down = load(w_gate[0], w_up[0], w_down[0])
    arrived[-1] = after(arrived[-1], gate)
    mine = jnp.concatenate(arrived, axis=0)
    far = ring_step(mine, "far_rows")

    apply = functools.partial(expert_apply, gate=gate, up=up, down=down)
    other = swap(mine)
    own_part, other_part = apply((1, 1), [mine, other])
    base = (own_part, swap(other_part))
    far, near = after(far, own_part), ring_step(other, "near_rows")
    near_terms, far_terms = [], []
    for k in range(1, half - 1):
        far_out, near_out, near_part, far_part = apply(
            (1, 1, 1, 1), [far, near, swap(far), swap(near)]
        )
        far = after(ring_step(far, "far_rows"), near, *(near_terms + far_terms)[-1:], *base)
        near = after(ring_step(near, "near_rows"), far_out)
        near_terms.append((near_part, swap(far_out)))
        far_terms.append((far_part, swap(near_out)))
    far_out, near_part = apply((1, 1), [far, swap(far)])
    far = after(ring_step(far, "far_rows"), near, far_out, *near_terms[-1], *far_terms[-1])
    near_terms.append((near_part, swap(far_out)))
    last_part, last_out = apply((1, 1), [after(far, *near_terms[-1]), swap(far)])
    far_sum = add(last_part, swap(last_out))
    near_out, far_part = apply((1, 1), [after(near, far_sum), swap(near)])
    far_terms.append((far_part, swap(near_out)))

    near_sum = None
    for k in range(half - 1, 0, -1):
        part, theirs = near_terms[k - 1]
        part = after(part, far_sum)
        near_sum = add(part, theirs) if near_sum is None else add(near_sum, part, theirs)
        near_sum = (ring_step if k > 1 else ring_leave)(near_sum, "near_sum")
        far_sum = add(ring_step(far_sum, "far_sum"), *far_terms[k - 1])
    slot_out = add(ring_step(far_sum, "far_sum"), near_sum, *base)

    here = jnp.concatenate(exchange(slot_out, -1), axis=0)
    far = tensor_step(here)
    near = swap(tensor_step(swap(here)))
    return collect(row_of, [here, near, tensor_step(far), far])


def solution(mesh):
    return jax.shard_map(
        per_device,
        mesh=mesh,
        in_specs=(
            P(("dp", "expert"), None),
            P(("dp", "expert"), None),
            P(),
            P(),
            P(("dp", "tensor"), None, "expert"),
            P(("dp", "tensor"), None, "expert"),
            P(("dp", "tensor"), "expert", None),
        ),
        out_specs=P(("dp", "expert"), None),
        check_vma=False,
    )
```

```python
import functools

import jax
import jax.numpy as jnp
from jax import lax
from jax.experimental import pallas as pl
from jax.experimental.pallas import tpu as pltpu
from jax.sharding import PartitionSpec as P

BF16 = jnp.bfloat16
F32 = jnp.float32
I32 = jnp.int32
LANES = 128
VMEM_LIMIT = 8 << 20


def in_vmem(values):
    return pltpu.with_memory_space_constraint(values, pltpu.VMEM)


def in_hbm(values):
    return pltpu.with_memory_space_constraint(values, pltpu.HBM)


def vmem_specs(count):
    return [pl.BlockSpec(memory_space=pltpu.VMEM)] * count


def step_of(size, most):
    return max(s for s in range(LANES, most + 1, LANES) if size % s == 0)


def add(*terms):
    total = terms[0].astype(F32)
    for term in terms[1:]:
        total = total + term.astype(F32)
    return total.astype(BF16)


def shift(values, axis, steps):
    size = lax.axis_size(axis)
    return lax.ppermute(values, axis, [(i, (i + steps) % size) for i in range(size)])


def ring_step(values, name):
    size = lax.axis_size("expert")
    pairs = [(i, (i + (2 if i % 2 == 0 else -2)) % size) for i in range(size)]
    with jax.named_scope(name):
        return lax.ppermute(values, "expert", pairs)


def ring_leave(values, name):
    size = lax.axis_size("expert")
    pairs = [(i, (i + (3 if i % 2 == 0 else -3)) % size) for i in range(size)]
    with jax.named_scope(name):
        return lax.ppermute(values, "expert", pairs)


def tensor_step(values):
    size, tensor_size = lax.axis_size("expert"), lax.axis_size("tensor")
    pairs = [
        (t * size + i, (t + (1 if i % 2 == 0 else -1)) % tensor_size * size + i)
        for t in range(tensor_size)
        for i in range(size)
    ]
    return lax.ppermute(values, ("tensor", "expert"), pairs)


def swap(values):
    size = lax.axis_size("expert")
    with jax.named_scope("other_core"):
        return lax.ppermute(values, "expert", [(i, i ^ 1) for i in range(size)])


def route_kernel(sizes, place, *refs):
    dp_size, tensor_size, capacity = sizes
    sources, row_of, packed = refs[:4], refs[4], refs[5]
    tokens, ids_row, gain, router, normed, sems = refs[6:]
    count, features = tokens.shape
    rows = packed.shape[0]
    step = step_of(features, 1280)
    spans = [pl.ds(i, step) for i in range(0, features, step)]
    part_size = step_of(features, 1280)
    part_spans = [pl.ds(i, part_size) for i in range(0, features, part_size)]
    copies = [
        pltpu.make_async_copy(source, held, sems.at[i])
        for i, (source, held) in enumerate(zip(sources[1:], (ids_row, gain, router)))
    ] + [
        pltpu.make_async_copy(sources[0].at[:, cols], tokens.at[:, cols], sems.at[3 + i])
        for i, cols in enumerate(part_spans)
    ]
    for copy in copies:
        copy.start()

    copies[0].wait()
    down = lax.broadcasted_iota(I32, (count, count), 0)
    across = lax.broadcasted_iota(I32, (count, count), 1)
    ids_col = jnp.sum(jnp.where(down == across, ids_row[...], 0), axis=1, keepdims=True)
    same = ids_col == ids_row[...]
    slot_col = jnp.sum(jnp.where(same & (across < down), 1, 0), axis=1, keepdims=True)
    slot_row = jnp.sum(jnp.where(same & (down < across), 1, 0), axis=0, keepdims=True)

    def ahead(ids):
        dp_of = jnp.zeros_like(ids)
        for d in range(1, dp_size):
            dp_of = dp_of + jnp.where(ids >= d * tensor_size, 1, 0)
        on_dp = dp_of - place[0]
        on_tensor = (ids - dp_of * tensor_size - place[1]) * place[2]
        on_dp = jnp.where(on_dp < 0, on_dp + dp_size, on_dp)
        return on_dp, jnp.where(on_tensor < 0, on_tensor + tensor_size, on_tensor)

    on_dp, on_tensor = ahead(ids_col)
    row_of[...] = (on_tensor * dp_size + on_dp) * capacity + slot_col
    on_dp, on_tensor = ahead(ids_row[...])
    target = jnp.where(on_tensor == 0, on_dp * capacity + slot_row, -1)
    row = lax.broadcasted_iota(I32, (rows, count), 0)
    picks = jnp.where(row == target, 1.0, 0.0).astype(BF16)

    total = jnp.zeros((rows, LANES), F32)
    for cols, copy in zip(part_spans, copies[3:]):
        copy.wait()
        part = jnp.dot(picks, tokens[:, cols], preferred_element_type=F32)
        normed[:, cols] = part.astype(BF16)
        for i in range(0, part_size, LANES):
            total = total + part[:, i : i + LANES] * part[:, i : i + LANES]
    scale = lax.rsqrt(jnp.sum(total, axis=1, keepdims=True) * (1.0 / features) + 1e-05)

    copies[1].wait()
    copies[2].wait()
    logits = jnp.zeros((rows, router.shape[0]), F32)
    for cols in spans:
        part = (normed[:, cols].astype(F32) * scale * gain[:, cols]).astype(BF16)
        normed[:, cols] = part
        logits = logits + lax.dot_general(
            part, router[:, cols], (((1,), (1,)), ((), ())), preferred_element_type=F32
        )
    row = lax.broadcasted_iota(I32, logits.shape, 0)
    dp_of = jnp.zeros_like(row) + place[0]
    for d in range(1, dp_size):
        dp_of = dp_of + jnp.where(row >= d * capacity, 1, 0)
    dp_of = jnp.where(dp_of >= dp_size, dp_of - dp_size, dp_of)
    expert = lax.broadcasted_iota(I32, logits.shape, 1)
    mine = expert == dp_of * tensor_size + place[1]
    chosen = jnp.sum(jnp.where(mine, logits, 0.0), axis=1, keepdims=True)
    gate = 1.0 / (1.0 + jnp.exp(-chosen))
    for cols in spans:
        packed[:, cols] = (normed[:, cols].astype(F32) * gate).astype(BF16)


def route(sizes, place, tokens, expert_ids, norm_gain, router_weight):
    count, features = tokens.shape
    dp_size, _, capacity = sizes
    operands = (
        tokens,
        expert_ids.reshape(1, count),
        norm_gain.reshape(1, features),
        router_weight.T,
    )
    return pl.pallas_call(
        functools.partial(route_kernel, sizes),
        out_shape=[
            pltpu.VMEM((count, 1), I32),
            pltpu.VMEM((dp_size * capacity, features), BF16),
        ],
        in_specs=[pl.BlockSpec(memory_space=pltpu.SMEM)]
        + [pl.BlockSpec(memory_space=pl.ANY)] * len(operands),
        out_specs=vmem_specs(2),
        scratch_shapes=[pltpu.VMEM(x.shape, x.dtype) for x in operands]
        + [
            pltpu.VMEM((dp_size * capacity, features), BF16),
            pltpu.SemaphoreType.DMA((3 + features // step_of(features, 1280),)),
        ],
        compiler_params=pltpu.CompilerParams(vmem_limit_bytes=VMEM_LIMIT),
    )(place, *map(in_hbm, operands))


def load_kernel(*refs):
    count = len(refs) // 2
    sems = refs[-1]
    copies = [
        pltpu.make_async_copy(refs[i], refs[count + i], sems.at[i]) for i in range(count)
    ]
    for copy in copies:
        copy.start()
    for copy in copies:
        copy.wait()


def load(*arrays):
    return pl.pallas_call(
        load_kernel,
        out_shape=[pltpu.VMEM(x.shape, x.dtype) for x in arrays],
        in_specs=[pl.BlockSpec(memory_space=pl.ANY)] * len(arrays),
        out_specs=vmem_specs(len(arrays)),
        scratch_shapes=[pltpu.SemaphoreType.DMA((len(arrays),))],
        compiler_params=pltpu.CompilerParams(vmem_limit_bytes=VMEM_LIMIT),
    )(*map(in_hbm, arrays))


def expert_kernel(groups, *refs):
    count = sum(groups)
    pieces, (gate, up, down), outs = refs[:count], refs[count : count + 3], refs[count + 3 : -2]
    acts, hidden = refs[-2:]
    features, units = gate.shape
    step = step_of(features, 2560)
    acts[...] = jnp.zeros_like(acts)

    @pl.loop(0, features // step)
    def _(i):
        cols = pl.ds(pl.multiple_of(i * step, step), step)
        rows = jnp.concatenate([piece[:, cols].astype(F32) for piece in pieces], axis=0)
        weights = jnp.concatenate([gate[cols, :], up[cols, :]], axis=1)
        acts[...] += jnp.dot(rows.astype(BF16), weights, preferred_element_type=F32)

    gate_act, up_act = acts[:, :units], acts[:, units:]
    hidden[...] = (gate_act / (1.0 + jnp.exp(-gate_act)) * up_act).astype(BF16)

    @pl.loop(0, features // step)
    def _(i):
        cols = pl.ds(pl.multiple_of(i * step, step), step)
        product = jnp.dot(hidden[...], down[:, cols], preferred_element_type=F32)
        first = 0
        for out in outs:
            out[:, cols] = product[first : first + out.shape[0]].astype(BF16)
            first += out.shape[0]


def expert_apply(groups, pieces, gate, up, down):
    rows, features = pieces[0].shape
    total = rows * sum(groups)
    units = gate.shape[1]
    operands = [in_vmem(x) for x in (*pieces, gate, up, down)]
    return pl.pallas_call(
        functools.partial(expert_kernel, groups),
        out_shape=[pltpu.VMEM((rows * n, features), BF16) for n in groups],
        in_specs=vmem_specs(len(operands)),
        out_specs=vmem_specs(len(groups)),
        scratch_shapes=[pltpu.VMEM((total, 2 * units), F32), pltpu.VMEM((total, units), BF16)],
        compiler_params=pltpu.CompilerParams(vmem_limit_bytes=VMEM_LIMIT),
    )(*operands)


def collect_kernel(row_of, *refs):
    pieces, (out, held, sems) = refs[:-3], refs[-3:]
    count, features = held.shape
    step = step_of(features, 1024)
    total = sum(piece.shape[0] for piece in pieces)
    across = lax.broadcasted_iota(I32, (count, total), 1)
    picks = jnp.where(row_of[...] == across, 1.0, 0.0).astype(BF16)
    copies = []
    for i in range(features // step):
        cols = pl.ds(i * step, step)
        rows = jnp.concatenate([piece[:, cols].astype(F32) for piece in pieces], axis=0)
        held[:, cols] = jnp.dot(picks, rows.astype(BF16), preferred_element_type=F32).astype(BF16)
        copies.append(pltpu.make_async_copy(held.at[:, cols], out.at[:, cols], sems.at[i]))
        copies[-1].start()
    for copy in copies:
        copy.wait()


def collect(row_of, pieces):
    count, features = row_of.shape[0], pieces[0].shape[1]
    return pl.pallas_call(
        collect_kernel,
        out_shape=jax.ShapeDtypeStruct((count, features), BF16),
        in_specs=vmem_specs(1 + len(pieces)),
        out_specs=pl.BlockSpec(memory_space=pl.ANY),
        scratch_shapes=[
            pltpu.VMEM((count, features), BF16),
            pltpu.SemaphoreType.DMA((features // step_of(features, 1024),)),
        ],
        compiler_params=pltpu.CompilerParams(vmem_limit_bytes=VMEM_LIMIT),
    )(*map(in_vmem, (row_of, *pieces)))


def exchange(values, direction):
    size = lax.axis_size("dp")
    rows = values.shape[0] // size
    blocks = [values[j * rows : (j + 1) * rows] for j in range(size)]
    return blocks[:1] + [shift(blocks[j], "dp", direction * j) for j in range(1, size)]


def after(values, *earlier):
    return lax.optimization_barrier((values, *earlier))[0]


def per_device(tokens, expert_ids, norm_gain, router_weight, w_gate, w_up, w_down):
    dp_size = lax.axis_size("dp")
    tensor_size = lax.axis_size("tensor")
    chips = lax.axis_size("expert") // 2
    half = chips // 2
    capacity = 5 * tokens.shape[0] // (4 * dp_size * tensor_size)
    rows = dp_size * capacity
    core = lax.axis_index("expert") % 2
    place = jnp.stack([lax.axis_index("dp"), lax.axis_index("tensor"), 1 - 2 * core]).astype(I32)

    row_of, packed = route(
        (dp_size, tensor_size, capacity), place, tokens, expert_ids, norm_gain, router_weight
    )
    arrived = exchange(packed, 1)
    gate, up, down = load(w_gate[0], w_up[0], w_down[0])
    arrived[-1] = after(arrived[-1], gate)
    mine = jnp.concatenate(arrived, axis=0)
    far = ring_step(mine, "far_rows")

    apply = functools.partial(expert_apply, gate=gate, up=up, down=down)
    other = swap(mine)
    own_part, other_part = apply((1, 1), [mine, other])
    base = (own_part, swap(other_part))
    far, near = after(far, own_part), ring_step(other, "near_rows")
    near_terms, far_terms = [], []
    for k in range(1, half - 1):
        far_out, near_out, near_part, far_part = apply(
            (1, 1, 1, 1), [far, near, swap(far), swap(near)]
        )
        far = after(ring_step(far, "far_rows"), near, *(near_terms + far_terms)[-1:], *base)
        near = after(ring_step(near, "near_rows"), far_out)
        near_terms.append((near_part, swap(far_out)))
        far_terms.append((far_part, swap(near_out)))
    far_out, near_part = apply((1, 1), [far, swap(far)])
    far = after(ring_step(far, "far_rows"), near, far_out, *near_terms[-1], *far_terms[-1])
    near_terms.append((near_part, swap(far_out)))
    last_part, last_out = apply((1, 1), [after(far, *near_terms[-1]), swap(far)])
    far_sum = add(last_part, swap(last_out))
    near_out, far_part = apply((1, 1), [after(near, far_sum), swap(near)])
    far_terms.append((far_part, swap(near_out)))

    near_sum = None
    for k in range(half - 1, 0, -1):
        part, theirs = near_terms[k - 1]
        part = after(part, far_sum) if near_sum is not None else after(part, far_part)
        near_sum = add(part, theirs) if near_sum is None else add(near_sum, part, theirs)
        near_sum = (ring_step if k > 1 else ring_leave)(near_sum, "near_sum")
        far_sum = add(ring_step(far_sum, "far_sum"), *far_terms[k - 1])
    slot_out = add(ring_step(far_sum, "far_sum"), near_sum, *base)

    here = jnp.concatenate(exchange(slot_out, -1), axis=0)
    far = tensor_step(here)
    near = swap(tensor_step(swap(here)))
    return collect(row_of, [here, near, tensor_step(far), far])


def solution(mesh):
    return jax.shard_map(
        per_device,
        mesh=mesh,
        in_specs=(
            P(("dp", "expert"), None),
            P(("dp", "expert"), None),
            P(),
            P(),
            P(("dp", "tensor"), None, "expert"),
            P(("dp", "tensor"), None, "expert"),
            P(("dp", "tensor"), "expert", None),
        ),
        out_specs=P(("dp", "expert"), None),
        check_vma=False,
    )
```
